32 devices in a mesh: seq: 8 (over z, x), tp: 4 (over y, core).
Axes of the slice: x: 2, y: 2, z: 4, core: 2. Of those that a mesh axis runs over, the one named last changes fastest.
Arguments:
- tokens: bfloat16 [2, 2048, 2048], P(None, 'seq'), may hold values from -6 to 6
- doc_lengths: int32 [2, 8], replicated, may hold values from 1 to 1948, as said below
- pad_mask: int32 [2, 2048], P(None, 'seq'), may hold values 0 or 1
- gain_mix: float32 [2048], replicated, may hold values from 0.25 to 1.75
- w_in: bfloat16 [2048, 3, 2048], P(None, None, 'tp'), may hold values from -0.125 to 0.125
- short_conv: float32 [3, 3, 2048], P(None, None, 'tp'), may hold values from -3 to 3
- pole_log_rate: float32 [16, 2048], P(None, 'tp'), may hold values from -14 to -2
- residue: float32 [16, 2048], P(None, 'tp'), may hold values from -2 to 2
- w_out: bfloat16 [2048, 2048], P('tp'), may hold values from -0.125 to 0.125
- gain_ffn: float32 [2048], replicated, may hold values from 0.25 to 1.75
- w_gu: bfloat16 [2048, 2, 5632], P(None, None, 'tp'), may hold values from -0.125 to 0.125
- w_down: bfloat16 [5632, 2048], P('tp'), may hold values from -0.15625 to 0.15625
- cotangent: bfloat16 [2, 2048, 2048], P(None, 'seq'), may hold values from -6 to 6
Outputs:
- block_out: bfloat16 [2, 2048, 2048], P(None, 'seq')
- grad_tokens: bfloat16 [2, 2048, 2048], P(None, 'seq')
- grad_gain_mix: float32 [2048], replicated
- grad_w_in: float32 [2048, 3, 2048], P('seq', None, 'tp')
- grad_short_conv: float32 [3, 3, 2048], P(None, None, 'tp')
- grad_pole_log_rate: float32 [16, 2048], P(None, 'tp')
- grad_residue: float32 [16, 2048], P(None, 'tp')
- grad_w_out: float32 [2048, 2048], P('tp', 'seq')
- grad_gain_ffn: float32 [2048], replicated
- grad_w_gu: float32 [2048, 2, 5632], P('seq', None, 'tp')
- grad_w_down: float32 [5632, 2048], P('tp', 'seq')
The draws below stay inside these ranges and needn't reach their ends.
Inputs may be any that keep to these rules, and one draw needn't show every extreme that they name: `doc_lengths`: each row's lengths sum to 2048. In row 0 one document, at a place drawn from the seed, begins within the first 256 tokens and ends within the last 256; each other one is 1 to 32 tokens long. In row 1 one document, at a place drawn from the seed, has exactly 512 tokens and every other one fewer.
All inputs are finite; a program needn't handle non-finite values. No bound on the sum of `pad_mask` on one device may be relied on, other than what follows from the above.
Results may differ from the reference program's by a relative error of at most 0.023.
Values may be sent and summed in bfloat16 or wider, within the bound.
A program may use at most 256 MiB of HBM per device.

```python
import math
import jax
import jax.numpy as jnp
from jax import lax

D = 2048
FF = 5632
POLES = 16
ROWS = 2
DOCS = 8
TOK_DEV = 256
TOKENS = 2048


def draw_doc_lengths(key, part):
    key = jax.random.fold_in(key, 5)
    first_key, second_key, third_key, fourth_key, fifth_key = jax.random.split(key, 5)
    most_short = TOK_DEV // DOCS
    paired = jax.random.randint(first_key, (DOCS,), 1, most_short + 1)
    longest = jax.random.randint(second_key, (), 0, DOCS)
    other_index = jnp.arange(DOCS - 1)
    pair_value = paired[other_index // 2]
    others = jnp.where(other_index % 2 == 0, pair_value, most_short + 1 - pair_value)
    if (DOCS - 1) % 2 == 1:
        others = jnp.where(other_index == DOCS - 2, 1, others)
    long_len = TOKENS - (DOCS - 1) // 2 * (most_short + 1) - (DOCS - 1) % 2
    indices = jnp.arange(DOCS)
    slot = jnp.clip(indices - (indices > longest).astype(jnp.int32), 0, DOCS - 2)
    first_row = jnp.where(indices == longest, long_len, others[slot]).astype(jnp.int32)
    quarter = TOKENS // 4
    pair_sum = quarter - 1
    top_bit = max(int(math.log2(pair_sum)), 1)
    bit_count = jax.random.randint(third_key, (3,), 0, top_bit + 1)
    spans = jax.random.randint(fourth_key, (3,), 0, jnp.left_shift(jnp.ones((3,), jnp.int32), bit_count))
    firsts = jnp.clip(1 + spans, 1, pair_sum - 1)
    pieces = jnp.concatenate([jnp.full((1,), quarter, jnp.int32), jnp.stack([firsts, pair_sum - firsts], axis=1).reshape(-1), jnp.full((1,), TOKENS - quarter - 3 * pair_sum, jnp.int32)]).astype(jnp.int32)
    order = jax.random.permutation(fifth_key, DOCS)
    second_row = pieces[order]
    return jnp.stack([first_row, second_row], axis=0).astype(jnp.int32)


def draw_pole_log_rate(key, part):
    key = jax.random.fold_in(key, 9)
    first_key, second_key = jax.random.split(key)
    slow_share = 0.5
    chooser = jax.random.uniform(first_key, (POLES, D), jnp.float32)
    spread = jax.random.uniform(second_key, (POLES, D), jnp.float32)
    slow_log = math.log(0.05 / TOKENS) + spread * math.log(40.0)
    fast_log = math.log(0.02) + spread * math.log(2.5)
    return jnp.where(chooser < slow_share, slow_log, fast_log).astype(jnp.float32)


def set_ends(entries, rng, low, top_value):
    spot = [jax.random.randint(jax.random.fold_in(rng, axis), (), 0, length) for axis, length in enumerate(entries.shape)]
    main_axis = entries.shape.index(max(entries.shape))
    beside = spot[:main_axis] + [(spot[main_axis] + 1) % entries.shape[main_axis]] + spot[main_axis + 1:]
    return entries.at[tuple(spot)].set(low).at[tuple(beside)].set(top_value)


def block_levels(key, shape, cuts, low, largest):
    gain = 1.0
    for axis_at, parts in cuts:
        draws = jax.random.uniform(jax.random.fold_in(jax.random.fold_in(key, 6), axis_at), (parts,), jnp.float32, low / len(cuts), largest / len(cuts))
        gain = gain * jnp.repeat(jnp.exp(draws), shape[axis_at] // parts).reshape((-1,) + (1,) * (len(shape) - 1 - axis_at))
    return gain


def scatter_about(stream_key, extent, deviation, most, cuts=(), kind=jnp.bfloat16):
    gain = block_levels(stream_key, extent, cuts, -0.22, 0.18) if cuts else 1.0
    values = jax.random.normal(stream_key, extent, jnp.float32) * deviation * gain
    return jnp.minimum(jnp.maximum(values, -most), most).astype(kind)


def setup_inputs(seed: int = 0) -> dict:
    streams_of = jax.random.split(jax.random.key(seed), 14)
    tokens = scatter_about(streams_of[0], (ROWS, TOKENS, D), 1.0, 6.0, ((1, 8),))
    doc_lengths = draw_doc_lengths(jax.random.fold_in(streams_of[13], 71), 0)
    pad_mask = set_ends((jax.random.randint(streams_of[2], (ROWS, TOKENS), 0, 8) < 7).astype(jnp.int32), jax.random.fold_in(streams_of[2], 1), 0, 1)
    gain_mix = jnp.clip(1.0 + 0.15 * jax.random.normal(streams_of[3], (D,), jnp.float32), 0.25, 1.75)
    w_in = scatter_about(streams_of[4], (D, 3, D), D ** -0.5, 0.125, ((2, 4),))
    short_conv = scatter_about(streams_of[5], (3, 3, D), 0.6, 3.0, ((2, 4),), jnp.float32)
    pole_log_rate = draw_pole_log_rate(jax.random.fold_in(streams_of[13], 71), 0)
    residue = scatter_about(streams_of[7], (POLES, D), 0.35, 2.0, ((1, 4),), jnp.float32)
    w_out = scatter_about(streams_of[8], (D, D), D ** -0.5, 0.125, ((0, 4),))
    gain_ffn = jnp.clip(1.0 + 0.15 * jax.random.normal(streams_of[9], (D,), jnp.float32), 0.25, 1.75)
    w_gu = scatter_about(streams_of[10], (D, 2, FF), D ** -0.5, 0.125, ((2, 4),))
    w_down = scatter_about(streams_of[11], (FF, D), (FF // 4) ** -0.5, 0.15625, ((0, 4),))
    cotangent = scatter_about(streams_of[12], (ROWS, TOKENS, D), 1.0, 6.0, ((1, 8),))
    return dict(tokens=tokens, doc_lengths=doc_lengths, pad_mask=pad_mask, gain_mix=gain_mix, w_in=w_in, short_conv=short_conv, pole_log_rate=pole_log_rate, residue=residue, w_out=w_out, gain_ffn=gain_ffn, w_gu=w_gu, w_down=w_down, cotangent=cotangent)


epsilon = 1e-06
conv_block = 64
highest = lax.Precision.HIGHEST

@jax.custom_vjp
def low(v):
    return lax.optimization_barrier(v.astype(jnp.bfloat16)).astype(jnp.float32)

@jax.custom_vjp
def low_back(v):
    return v

def low_keep(v):
    return (low(v), None)

def low_pass(kept, grad):
    return (grad,)

def back_keep(v):
    return (v, None)

def back_low(kept, grad):
    return (low(grad),)
low.defvjp(low_keep, low_pass)
low_back.defvjp(back_keep, back_low)

def rms_norm(values, gain_vec):
    return values * lax.rsqrt(lax.optimization_barrier(jnp.mean(values * values, axis=-1, keepdims=True)) + epsilon) * gain_vec

def doc_begin(places, begins):
    return lax.optimization_barrier(jnp.max(jnp.where(begins[None, :] <= places[:, None], begins[None, :], 0), axis=1)).astype(jnp.int32)

def short_filter(projected, filter_taps, begin_tok, places):
    summed = jnp.zeros(projected.shape, jnp.float32)
    for tap_index in range(3):
        shifted = jnp.pad(projected, ((0, 0), (tap_index, 0), (0, 0), (0, 0)))[:, :projected.shape[1]]
        allowed = (begin_tok <= places[None, :] - tap_index).astype(jnp.float32)
        summed = summed + filter_taps[:, tap_index, :][None, None] * shifted * allowed[:, :, None, None]
    return summed

def modal_scan(values, log_rate, residue_in, state_start, begin_tok, places):
    decay_rate = jnp.exp(log_rate)
    pole_weight = residue_in * jnp.sqrt(decay_rate)
    offsets = jnp.arange(conv_block).astype(jnp.int32)
    offset_f = offsets.astype(jnp.float32)
    decay_table = jnp.exp(-decay_rate[None] * offset_f[:, None, None])
    response = low(jnp.einsum('qpd,pd->qd', decay_table, pole_weight, precision=highest))
    lag_grid = offsets[:, None] - offsets[None, :]
    toeplitz = jnp.where((lag_grid >= 0)[:, :, None], response[jnp.clip(lag_grid, 0, conv_block - 1)], 0.0)
    reversed_decay = decay_table[::-1]
    onward = jnp.exp(-decay_rate[None] * (offset_f[:, None, None] + 1.0))
    through = jnp.exp(-decay_rate * float(conv_block))

    def advance(carry_state, inputs):
        block_values, block_begin, block_places = inputs
        same_doc = (block_begin[:, None] <= block_places[None, :]).astype(jnp.float32)
        result = jnp.einsum('tsd,ts,sd->td', toeplitz, same_doc, block_values, precision=highest)
        carried = (block_begin < block_places[0]).astype(jnp.float32)
        result = result + carried[:, None] * jnp.einsum('qpd,pd->qd', onward, pole_weight * carry_state, precision=highest)
        tail_mask = (block_places >= block_begin[-1]).astype(jnp.float32)
        inner_state = jnp.einsum('qpd,qd->pd', reversed_decay, block_values * tail_mask[:, None], precision=highest)
        passing = (block_begin[-1] < block_places[0]).astype(jnp.float32)
        return (carry_state * through * passing + inner_state, result)
    blocks = values.shape[0] // conv_block
    results = lax.scan(jax.checkpoint(advance), state_start, (values.reshape(blocks, conv_block, values.shape[1]), begin_tok.reshape(blocks, conv_block), places.reshape(blocks, conv_block)))[1]
    return results.reshape(values.shape)

def reference(tokens, doc_lengths, pad_mask, gain_mix, w_in, short_conv, pole_log_rate, residue, w_out, gain_ffn, w_gu, w_down, cotangent):
    doc_ends = jnp.cumsum(doc_lengths, axis=1).astype(jnp.int32)
    begins = (doc_ends - doc_lengths).astype(jnp.int32)
    places = jnp.arange(tokens.shape[1]).astype(jnp.int32)
    begin_tok = jax.vmap(doc_begin, in_axes=(None, 0))(places, begins)
    keep_mask = pad_mask.astype(jnp.float32)

    def forward(inputs_f, gain_a, proj_w, filter_taps, log_rate, residue_w, out_w, gain_b, gate_up_w, down_w):
        normed = low(rms_norm(inputs_f, gain_a))
        projected = low(low_back(jnp.einsum('btd,dkc->btkc', normed, proj_w, precision=highest)))
        mixed_qkv = short_filter(projected, filter_taps, begin_tok, places)
        values = low(mixed_qkv[:, :, 1] * mixed_qkv[:, :, 2] * keep_mask[:, :, None])
        zero_state = jnp.zeros(log_rate.shape, jnp.float32)
        conv_out = low_back(jax.vmap(modal_scan, in_axes=(0, None, None, None, 0, None))(values, log_rate, residue_w, zero_state, begin_tok, places))
        gated_out = low(low_back(mixed_qkv[:, :, 0] * conv_out))
        middle = inputs_f + low_back(jnp.einsum('btc,cd->btd', gated_out, out_w, precision=highest))
        normed_b = low(rms_norm(middle, gain_b))
        gate_up = low_back(jnp.einsum('btd,dkf->btkf', normed_b, gate_up_w, precision=highest))
        hidden = low(jax.nn.silu(gate_up[:, :, 0]) * gate_up[:, :, 1])
        return middle + low_back(jnp.einsum('btf,fd->btd', hidden, down_w, precision=highest))
    result, pull_back = jax.vjp(forward, tokens.astype(jnp.float32), gain_mix, w_in.astype(jnp.float32), short_conv, pole_log_rate, residue, w_out.astype(jnp.float32), gain_ffn, w_gu.astype(jnp.float32), w_down.astype(jnp.float32))
    grads = pull_back(cotangent.astype(jnp.float32))
    return (result.astype(jnp.bfloat16), grads[0].astype(jnp.bfloat16), grads[1], grads[2], grads[3], grads[4], grads[5], grads[6], grads[7], grads[8], grads[9])
```

```python
import functools

import jax
import jax.numpy as jnp
from jax import lax
from jax.experimental import pallas as pl
from jax.experimental.pallas import tpu as pltpu
from jax.sharding import PartitionSpec as P

MESH = pl.DeviceIdType.MESH
epsilon = 1e-06
f32 = jnp.float32
bf16 = jnp.bfloat16
GROUP = 8
CHUNK = 32
TP_CHUNKS = 8


def doc_begin(places, begins):
    return jnp.max(jnp.where(begins[None, :] <= places[:, None], begins[None, :], 0), axis=1)


def rms_parts(values):
    inverse = lax.rsqrt(jnp.mean(values * values, axis=-1, keepdims=True) + epsilon)
    return (values * inverse, inverse)


def rms_back(grad_norm, gain_vec, unit_vec, inverse):
    scaled = grad_norm * gain_vec
    return inverse * (scaled - unit_vec * jnp.mean(scaled * unit_vec, axis=-1, keepdims=True))


def dot_nn(a, b):
    return lax.dot_general(a, b, (((1,), (0,)), ((), ())), preferred_element_type=f32)


def dot_nt(a, b):
    return lax.dot_general(a, b, (((1,), (1,)), ((), ())), preferred_element_type=f32)


def dot_tn(a, b):
    return lax.dot_general(a, b, (((0,), (0,)), ((), ())), preferred_element_type=f32)


def spread_kernel(count, own_ref, all_ref, send_sem, recv_sem, local_sem):
    me = lax.axis_index("seq")
    barrier = pltpu.get_barrier_semaphore()

    def greet(step, carry):
        pl.semaphore_signal(
            barrier, inc=1, device_id={"seq": lax.rem(me + step, count)}, device_id_type=MESH
        )
        return carry

    lax.fori_loop(1, count, greet, 0)
    pl.semaphore_wait(barrier, count - 1)
    local = pltpu.make_async_copy(own_ref, all_ref.at[me], local_sem)
    local.start()

    def copy(step, slot):
        return pltpu.make_async_remote_copy(
            src_ref=own_ref,
            dst_ref=all_ref.at[slot],
            send_sem=send_sem.at[step],
            recv_sem=recv_sem.at[step],
            device_id={"seq": lax.rem(me + step, count)},
            device_id_type=MESH,
        )

    def send(step, carry):
        copy(step, me).start()
        return carry

    lax.fori_loop(1, count, send, 0)
    local.wait()

    def finish(step, carry):
        arrived = copy(step, lax.rem(me + count - step, count))
        arrived.wait_send()
        arrived.wait_recv()
        return carry

    lax.fori_loop(1, count, finish, 0)


def spread(own, count, call_id):
    return pl.pallas_call(
        functools.partial(spread_kernel, count),
        out_shape=jax.ShapeDtypeStruct((count,) + own.shape, own.dtype),
        in_specs=[pl.BlockSpec(memory_space=pltpu.VMEM)],
        out_specs=pl.BlockSpec(memory_space=pltpu.VMEM),
        scratch_shapes=[
            pltpu.SemaphoreType.DMA((count,)),
            pltpu.SemaphoreType.DMA((count,)),
            pltpu.SemaphoreType.DMA,
        ],
        compiler_params=pltpu.CompilerParams(collective_id=call_id, has_side_effects=True),
    )(own)


def widen(mask, channels):
    return jnp.concatenate([mask] * (channels // mask.shape[-1]), axis=-1)


def conv_start_kernel(proj_ref, halo_ref, taps_ref, rate_ref, mask_ref, query_ref, mixed_ref, values_ref, end_ref, pad_ref):
    rows, tokens, channels = values_ref.shape
    poles = rate_ref.shape[0]
    for k in range(3):
        for row in range(rows):
            pad_ref[row, 0:8] = halo_ref[k, row].astype(f32)
            pad_ref[row, 8:] = proj_ref[k, row].astype(f32)
        for row in range(rows):
            for first in range(0, tokens, CHUNK):
                total = taps_ref[k, 0:1] * pad_ref[row, 8 + first : 8 + first + CHUNK]
                for tap in (1, 2):
                    allowed = widen(mask_ref[tap, row, first : first + CHUNK], channels)
                    begin = 8 - tap + first
                    total = total + taps_ref[k, tap : tap + 1] * pad_ref[row, begin : begin + CHUNK] * allowed
                if k == 0:
                    query_ref[row, first : first + CHUNK] = total
                else:
                    mixed_ref[k - 1, row, first : first + CHUNK] = total
                if k == 2:
                    keep = widen(mask_ref[0, row, first : first + CHUNK], channels)
                    product = mixed_ref[0, row, first : first + CHUNK] * total * keep
                    values_ref[row, first : first + CHUNK] = product.astype(bf16).astype(f32)
    decay = jnp.exp(-jnp.exp(rate_ref[...]))

    def step(group, states):
        for offset in range(GROUP):
            at = group * GROUP + offset
            states = tuple(
                states[row] * decay
                + values_ref[row, pl.ds(at, 1)] * widen(mask_ref[3, row, pl.ds(at, 1)], channels)
                for row in range(rows)
            )
        return states

    zero = jnp.zeros((poles, channels), f32)
    ends = lax.fori_loop(0, tokens // GROUP, step, (zero,) * rows)
    for row in range(rows):
        end_ref[row] = ends[row].astype(bf16)


def carried_state(all_ref, carry_ref, row, order, decay_far, shape):
    state = jnp.zeros(shape, f32)
    for position in order:
        advance = carry_ref[2 * row + 1, position]
        state = state * (1.0 + advance * (decay_far - 1.0)) + all_ref[position, row].astype(f32) * carry_ref[2 * row, position]
    return state


def conv_forward_kernel(values_ref, query_ref, all_ref, carry_ref, rate_ref, residue_ref, mask_ref, conv_ref, gated_ref, begin_ref):
    rows, tokens, channels = values_ref.shape
    poles = rate_ref.shape[0]
    rate = jnp.exp(rate_ref[...])
    decay = jnp.exp(-rate)
    decay_far = jnp.exp(-rate * float(tokens))
    weight = residue_ref[...] * jnp.sqrt(rate)
    starts = []
    for row in range(rows):
        start = carried_state(all_ref, carry_ref, row, range(all_ref.shape[0]), decay_far, (poles, channels))
        begin_ref[row] = start
        starts.append(start)

    def step(group, states):
        for offset in range(GROUP):
            at = group * GROUP + offset
            following = []
            for row in range(rows):
                same = widen(mask_ref[1, row, pl.ds(at, 1)], channels)
                state = states[row] * (decay * same) + values_ref[row, pl.ds(at, 1)]
                conv_ref[row, pl.ds(at, 1)] = jnp.sum(state * weight, axis=0, keepdims=True)
                following.append(state)
            states = tuple(following)
        return states

    lax.fori_loop(0, tokens // GROUP, step, tuple(starts))
    for row in range(rows):
        for first in range(0, tokens, CHUNK):
            part = slice(first, first + CHUNK)
            gated_ref[row, part] = (query_ref[row, part] * conv_ref[row, part]).astype(bf16)


def conv_back_start_kernel(grad_gated_ref, query_ref, rate_ref, mask_ref, grad_conv_ref, head_ref):
    rows, tokens, channels = query_ref.shape
    poles = rate_ref.shape[0]
    for row in range(rows):
        for first in range(0, tokens, CHUNK):
            part = slice(first, first + CHUNK)
            product = grad_gated_ref[row, part].astype(f32) * query_ref[row, part]
            grad_conv_ref[row, part] = product.astype(bf16).astype(f32)
    decay = jnp.exp(-jnp.exp(rate_ref[...]))

    def step(group, states):
        for offset in range(GROUP):
            at = tokens - 1 - (group * GROUP + offset)
            states = tuple(
                states[row] * decay
                + grad_conv_ref[row, pl.ds(at, 1)] * widen(mask_ref[4, row, pl.ds(at, 1)], channels)
                for row in range(rows)
            )
        return states

    zero = jnp.zeros((poles, channels), f32)
    heads = lax.fori_loop(0, tokens // GROUP, step, (zero,) * rows)
    for row in range(rows):
        head_ref[row] = heads[row].astype(bf16)


def conv_back_kernel(
    values_ref,
    grad_conv_ref,
    grad_gated_ref,
    mixed_ref,
    conv_ref,
    proj_ref,
    halo_ref,
    taps_ref,
    begin_ref,
    all_ref,
    carry_ref,
    rate_ref,
    residue_ref,
    mask_ref,
    grad_proj_ref,
    front_ref,
    grad_taps_ref,
    grad_rate_ref,
    grad_residue_ref,
    history_ref,
    grad_values_ref,
    pad_ref,
    padded_ref,
):
    rows, tokens, channels = values_ref.shape
    poles = rate_ref.shape[0]
    count = all_ref.shape[0]
    rate = jnp.exp(rate_ref[...])
    decay = jnp.exp(-rate)
    decay_far = jnp.exp(-rate * float(tokens))
    root = jnp.sqrt(rate)
    weight = residue_ref[...] * root
    shape = (poles, channels)
    zero = jnp.zeros(shape, f32)
    grad_residue_ref[...] = zero
    grad_rate_ref[...] = zero
    for row in range(rows):

        def ahead(group, carry):
            state, total = carry
            for offset in range(GROUP):
                at = group * GROUP + offset
                same = widen(mask_ref[1, row, pl.ds(at, 1)], channels)
                history_ref[at] = state
                state = state * (decay * same) + values_ref[row, pl.ds(at, 1)]
                total = total + state * grad_conv_ref[row, pl.ds(at, 1)]
            return state, total

        total = lax.fori_loop(0, tokens // GROUP, ahead, (begin_ref[row], zero))[1]

        def behind(group, carry):
            incoming, cross = carry
            for offset in range(GROUP):
                at = tokens - 1 - (group * GROUP + offset)
                same = widen(mask_ref[1, row, pl.ds(at, 1)], channels)
                state = incoming + grad_conv_ref[row, pl.ds(at, 1)]
                grad_values_ref[row, pl.ds(at, 1)] = jnp.sum(state * weight, axis=0, keepdims=True)
                incoming = state * (decay * same)
                cross = cross + incoming * history_ref[at]
            return incoming, cross

        start = carried_state(all_ref, carry_ref, row, range(count - 1, -1, -1), decay_far, shape)
        cross = lax.fori_loop(0, tokens // GROUP, behind, (start * decay, zero))[1]
        grad_residue_ref[...] += root * total
        grad_rate_ref[...] += weight * (0.5 * total - rate * cross)

    for k in range(3):
        for row in range(rows):
            pad_ref[row, 0:8] = halo_ref[k, row].astype(f32)
            pad_ref[row, 8:] = proj_ref[k, row].astype(f32)
            padded_ref[row, 0:8] = jnp.zeros((8, channels), f32)
        sums = [jnp.zeros((1, channels), f32) for tap in range(3)]
        for row in range(rows):
            for first in range(0, tokens, CHUNK):
                part = slice(first, first + CHUNK)
                if k == 0:
                    grad_mixed = grad_gated_ref[row, part].astype(f32) * conv_ref[row, part]
                else:
                    keep = widen(mask_ref[0, row, part], channels)
                    grad_mixed = grad_values_ref[row, part] * mixed_ref[2 - k, row, part] * keep
                padded_ref[row, 8 + first : 8 + first + CHUNK] = taps_ref[k, 0:1] * grad_mixed
                sums[0] = sums[0] + jnp.sum(
                    grad_mixed * pad_ref[row, 8 + first : 8 + first + CHUNK], axis=0, keepdims=True
                )
                for tap in (1, 2):
                    begin = 8 - tap + first
                    allowed = grad_mixed * widen(mask_ref[tap, row, part], channels)
                    padded_ref[row, begin : begin + CHUNK] += taps_ref[k, tap : tap + 1] * allowed
                    sums[tap] = sums[tap] + jnp.sum(
                        allowed * pad_ref[row, begin : begin + CHUNK], axis=0, keepdims=True
                    )
            grad_proj_ref[k, row] = padded_ref[row, 8:]
            front_ref[k, row] = padded_ref[row, 0:8]
        for tap in range(3):
            grad_taps_ref[k, tap : tap + 1] = sums[tap]


def vmem_call(kernel, outs, scratch, smem_at, *operands):
    specs = [
        pl.BlockSpec(memory_space=pltpu.SMEM if at in smem_at else pltpu.VMEM)
        for at in range(len(operands))
    ]
    return pl.pallas_call(
        kernel,
        out_shape=[jax.ShapeDtypeStruct(shape, kind) for shape, kind in outs],
        in_specs=specs,
        out_specs=[pl.BlockSpec(memory_space=pltpu.VMEM)] * len(outs),
        scratch_shapes=scratch,
        compiler_params=pltpu.CompilerParams(vmem_limit_bytes=48 * 1024 * 1024),
    )(*operands)


def tp_sum_kernel(finish, extras, gains, outs, zeroed, swaps, count, small, lines, part_ref, *refs):
    line_refs, refs = refs[:lines], refs[lines:]
    pair_count = sum(swaps)
    if small:
        small_ref, refs = refs[0], refs[1:]
    swap_refs, refs = refs[: len(swaps)], refs[len(swaps) :]
    far_refs = refs[:extras]
    gain_refs = refs[extras : extras + gains]
    out_refs = refs[extras + gains : extras + gains + outs]
    pair_refs = refs[extras + gains + outs : extras + gains + outs + pair_count]
    scratch = refs[extras + gains + outs + pair_count :]
    if small:
        all_ref, scratch = scratch[0], scratch[1:]
    line_outs, scratch = scratch[:lines], scratch[lines:]
    if lines:
        (line_acc, line_got, line_sent, line_came), scratch = scratch[-4:], scratch[:-4]
    if small:
        scratch, spread_sems = scratch[:-2], scratch[-2:]
    near_refs, scratch = scratch[:extras], scratch[extras:]
    total_ref, recv_a, half_ref, recv_b, load_sem, sent_a, got_a, sent_b, got_b, sent_c, got_c, *swap_sems = scratch
    rows = part_ref.shape[0]
    half = rows // 2
    chunk = half // TP_CHUNKS
    me = lax.axis_index("tp")
    core = lax.rem(me, 2)
    near = me + 1 - 2 * core
    far = lax.rem(me + 2, 4)
    own = core * half
    other = half - own
    for at in zeroed:
        out_refs[at][...] = jnp.zeros(out_refs[at].shape, out_refs[at].dtype)
    loads = [
        pltpu.make_async_copy(source, target, load_sem.at[at])
        for at, (source, target) in enumerate(zip(far_refs, near_refs))
    ]
    for load in loads:
        load.start()
    place_seq = lax.axis_index("seq")
    parity = lax.rem(place_seq, 2)
    mate = place_seq + 1 - 2 * parity
    keeps, exchanges, forwards = [], [], []
    sources = []
    for source, stacked in zip(swap_refs, swaps):
        sources += [source] if stacked == 1 else [source.at[at] for at in range(stacked)]
    for at, (source, target) in enumerate(zip(sources, pair_refs)):
        height, extent = source.shape
        sliced = target.shape[1] < extent
        lower, upper = pl.ds(0, height), pl.ds(height, height)
        if not sliced:
            keeps.append(pltpu.make_async_copy(source, target.at[lower], swap_sems[0].at[at, 0]))
            exchanges.append(
                pltpu.make_async_remote_copy(
                    src_ref=source,
                    dst_ref=target.at[upper],
                    send_sem=swap_sems[1].at[at, 0],
                    recv_sem=swap_sems[2].at[at, 0],
                    device_id={"seq": mate},
                    device_id_type=MESH,
                )
            )
            continue
        wide = extent // count
        half_pieces = count // 4

        def columns(which):
            return pl.ds(pl.multiple_of(which * wide, wide), wide)

        for piece in range(2 * half_pieces):
            keeps.append(
                pltpu.make_async_copy(
                    source.at[:, columns(2 * piece + parity)],
                    target.at[lower, pl.ds(piece * wide, wide)],
                    swap_sems[0].at[at, piece],
                )
            )
        for piece in range(half_pieces):
            mine = core * half_pieces + piece
            theirs = half_pieces - core * half_pieces + piece
            exchanges.append(
                pltpu.make_async_remote_copy(
                    src_ref=source.at[:, columns(2 * mine + 1 - parity)],
                    dst_ref=target.at[upper, columns(mine)],
                    send_sem=swap_sems[1].at[at, piece],
                    recv_sem=swap_sems[2].at[at, piece],
                    device_id={"seq": mate},
                    device_id_type=MESH,
                )
            )

            def hand_on(which, at=at, piece=piece, target=target, upper=upper, columns=columns):
                return pltpu.make_async_remote_copy(
                    src_ref=target.at[upper, columns(which)],
                    dst_ref=target.at[upper, columns(which)],
                    send_sem=swap_sems[3].at[at, piece],
                    recv_sem=swap_sems[4].at[at, piece],
                    device_id={"tp": near},
                    device_id_type=MESH,
                )

            forwards.append((exchanges[-1], hand_on(mine), hand_on(theirs)))
    barrier = pltpu.get_barrier_semaphore()
    for device in (near, far):
        pl.semaphore_signal(barrier, inc=1, device_id={"tp": device}, device_id_type=MESH)
    if swaps:
        pl.semaphore_signal(barrier, inc=1, device_id={"seq": mate}, device_id_type=MESH)
    if lines and not small:
        for offset in (2, count - 2):
            device = lax.rem(place_seq + offset, count)
            pl.semaphore_signal(barrier, inc=1, device_id={"seq": device}, device_id_type=MESH)
    if small:

        def greet(step, carry):
            device = lax.rem(place_seq + step, count)
            pl.semaphore_signal(barrier, inc=1, device_id={"seq": device}, device_id_type=MESH)
            return carry

        lax.fori_loop(1, count, greet, 0)
    greeted = count - 1 if small else 2 if lines else 0
    pl.semaphore_wait(barrier, 2 + (1 if swaps else 0) + greeted)

    def spread_copy(step, slot):
        return pltpu.make_async_remote_copy(
            src_ref=small_ref,
            dst_ref=all_ref.at[slot],
            send_sem=spread_sems[0].at[step],
            recv_sem=spread_sems[1].at[step],
            device_id={"seq": lax.rem(place_seq + step, count)},
            device_id_type=MESH,
        )

    if small:

        def send_small(step, carry):
            spread_copy(step, place_seq).start()
            return carry

        lax.fori_loop(1, count, send_small, 0)
        all_ref[place_seq] = small_ref[...]

    size = count // 2
    spot = place_seq // 2

    def along(way):
        return spot if way == 0 else size - 1 - spot

    def line_piece(unit, which):
        height = line_refs[unit].shape[0] // size
        return line_refs[unit].at[pl.ds(pl.multiple_of(which * height, height), height)]

    def line_copy(unit, way, step):
        source = line_piece(unit, (1 - way) * (size - 1)) if step == 1 else line_acc.at[unit, way, step - 2]
        return pltpu.make_async_remote_copy(
            src_ref=source,
            dst_ref=line_got.at[unit, way, step - 1],
            send_sem=line_sent.at[unit, way, step - 1],
            recv_sem=line_came.at[unit, way, step - 1],
            device_id={"seq": lax.rem(place_seq + (2, count - 2)[way], count)},
            device_id_type=MESH,
        )

    def sends(way, step):
        return along(way) <= min(step - 1, size - 2)

    def takes(way, step):
        return jnp.logical_and(along(way) >= 1, along(way) <= step)

    def line_send(step):
        for unit in range(lines):
            for way in range(2):

                @pl.when(sends(way, step))
                def _(unit=unit, way=way):
                    line_copy(unit, way, step).start()

    def line_take(step):
        for unit in range(lines):
            for way in range(2):

                @pl.when(takes(way, step))
                def _(unit=unit, way=way):
                    line_copy(unit, way, step).wait_recv()

                if step < size - 1:
                    ahead = (size - step - 1, step + 1)[way]
                    piece = line_piece(unit, lax.rem(spot + ahead, size))

                    @pl.when(takes(way, step))
                    def _(unit=unit, way=way, piece=piece):
                        added = line_got[unit, way, step - 1].astype(f32) + piece[...].astype(f32)
                        line_acc[unit, way, step - 1] = added.astype(bf16)

                    @pl.when(along(way) == 0)
                    def _(unit=unit, way=way, piece=piece):
                        line_acc[unit, way, step - 1] = piece[...]

    def line_advance(step):
        if lines and step < size - 1:
            line_take(step)
            line_send(step + 1)

    def span(base, at, size=chunk):
        return pl.ds(pl.multiple_of(base + at * size, size), size)

    def first(at, source):
        return pltpu.make_async_remote_copy(
            src_ref=part_ref.at[span(source, at)],
            dst_ref=recv_a.at[span(0, at)],
            send_sem=sent_a.at[at],
            recv_sem=got_a.at[at],
            device_id={"tp": near},
            device_id_type=MESH,
        )

    def second(at):
        return pltpu.make_async_remote_copy(
            src_ref=half_ref.at[span(0, at)],
            dst_ref=recv_b.at[span(0, at)],
            send_sem=sent_b.at[at],
            recv_sem=got_b.at[at],
            device_id={"tp": far},
            device_id_type=MESH,
        )

    def third(at, base):
        return pltpu.make_async_remote_copy(
            src_ref=total_ref.at[span(base, at)],
            dst_ref=total_ref.at[span(base, at)],
            send_sem=sent_c.at[at],
            recv_sem=got_c.at[at],
            device_id={"tp": near},
            device_id_type=MESH,
        )

    def apply(base, at):
        for inner in range(chunk // 16):
            place = pl.ds(pl.multiple_of(base + at * chunk + inner * 16, 16), 16)
            finish(
                total_ref[place].astype(f32),
                [ref[place].astype(f32) for ref in near_refs],
                [ref[...] for ref in gain_refs],
                out_refs,
                place,
            )

    def send_first(at, carry):
        first(at, other).start()
        return carry

    lax.fori_loop(0, TP_CHUNKS, send_first, 0)
    if lines and size > 1:
        line_send(1)

    def send_second(at, carry):
        first(at, other).wait_recv()
        summed = part_ref[span(own, at)].astype(f32) + recv_a[span(0, at)].astype(f32)
        half_ref[span(0, at)] = summed.astype(bf16)
        second(at).start()
        return carry

    lax.fori_loop(0, TP_CHUNKS, send_second, 0)
    for copy in exchanges + keeps:
        copy.start()
    line_advance(1)
    for load in loads:
        load.wait()

    def send_third(at, carry):
        second(at).wait_recv()
        summed = half_ref[span(0, at)].astype(f32) + recv_b[span(0, at)].astype(f32)
        total_ref[span(own, at)] = summed.astype(bf16)
        third(at, own).start()
        apply(own, at)
        return carry

    lax.fori_loop(0, TP_CHUNKS // 2, send_third, 0)
    line_advance(2)
    lax.fori_loop(TP_CHUNKS // 2, TP_CHUNKS, send_third, 0)
    for exchange, onward, _ in forwards:
        exchange.wait_recv()
        onward.start()

    def take_third(at, carry):
        third(at, other).wait_recv()
        apply(other, at)
        return carry

    lax.fori_loop(0, TP_CHUNKS, take_third, 0)

    for step in range(3, size - 1):
        line_advance(step)
    if lines and size > 1:
        line_take(size - 1)
    for unit in range(lines):
        line_outs[unit][...] = line_piece(unit, spot)[...].astype(f32)
        for way in range(2 if size > 1 else 0):

            @pl.when(along(way) >= 1)
            def _(unit=unit, way=way):
                line_outs[unit][...] += line_got[unit, way, size - 2].astype(f32)

            for step in range(1, size):

                @pl.when(sends(way, step))
                def _(unit=unit, way=way, step=step):
                    line_copy(unit, way, step).wait_send()

    def drain(at, carry):
        first(at, other).wait_send()
        second(at).wait_send()
        third(at, own).wait_send()
        return carry

    lax.fori_loop(0, TP_CHUNKS, drain, 0)
    for copy in keeps:
        copy.wait()
    handed = [id(exchange) for exchange, _, _ in forwards]
    for copy in exchanges:
        copy.wait_send()
        if id(copy) not in handed:
            copy.wait_recv()
    for _, onward, inward in forwards:
        onward.wait_send()
        inward.wait_recv()
    if small:

        def finish_small(step, carry):
            arrived = spread_copy(step, lax.rem(place_seq + count - step, count))
            arrived.wait_send()
            arrived.wait_recv()
            return carry

        lax.fori_loop(1, count, finish_small, 0)


def tp_sum(finish, call_id, part, extras, gains, outs, zeroed=(), swaps=(), count=2, small=None, lines=()):
    rows, width = part.shape
    vmem = pl.BlockSpec(memory_space=pltpu.VMEM)
    anywhere = pl.BlockSpec(memory_space=pl.ANY)
    parity = lax.rem(lax.axis_index("seq"), 2)
    if any(one[1] and (count % 4 or one[0].shape[1] // count % 128) for one in swaps):
        swap = [(i, i ^ 1) for i in range(count)]
        after = []
        for array, sliced in swaps:
            own, send = by_parity(array, count, parity, 1) if sliced else (array, array)
            after.append(jnp.concatenate([own, lax.ppermute(send, "seq", swap)], axis=0))
        results = tp_sum(
            finish, call_id, part, extras, gains, outs, zeroed, (), count, small, lines
        )
        return [*results[: len(outs)], *after, *results[len(outs) :]]
    pairs, stacked = [], []
    for array, sliced in swaps:
        height, extent = array.shape[-2:]
        stacked.append(array.shape[0] if array.ndim == 3 else 1)
        pair = jax.ShapeDtypeStruct((2 * height, extent // (2 if sliced else 1)), array.dtype)
        pairs += [pair] * stacked[-1]
    swap_sems = [pltpu.SemaphoreType.DMA((len(pairs), max(count // 2, 1)))] * 5 if swaps else []
    smalls = [] if small is None else [small]
    slots = max(count // 2 - 1, 1)
    summed, line_scratch = [], []
    if lines:
        height, extent = lines[0].shape
        height = height // (count // 2)
        summed = [jax.ShapeDtypeStruct((height, extent), f32)] * len(lines)
        line_scratch = [pltpu.VMEM((len(lines), 2, slots, height, extent), bf16)] * 2
        line_scratch = line_scratch + [pltpu.SemaphoreType.DMA((len(lines), 2, slots))] * 2
    gathered = [jax.ShapeDtypeStruct((count,) + one.shape, one.dtype) for one in smalls]
    return pl.pallas_call(
        functools.partial(tp_sum_kernel, finish, len(extras), len(gains), len(outs), zeroed, tuple(stacked), count, bool(smalls), len(lines)),
        out_shape=[jax.ShapeDtypeStruct(shape, kind) for shape, kind in outs] + pairs + gathered + summed,
        in_specs=[vmem] * (1 + len(lines) + len(smalls)) + [anywhere] * (len(swaps) + len(extras)) + [vmem] * len(gains),
        out_specs=[vmem] * len(outs) + [anywhere] * len(pairs) + [vmem] * (len(smalls) + len(lines)),
        scratch_shapes=[pltpu.VMEM(extra.shape, extra.dtype) for extra in extras]
        + [
            pltpu.VMEM((rows, width), bf16),
            pltpu.VMEM((rows // 2, width), bf16),
            pltpu.VMEM((rows // 2, width), bf16),
            pltpu.VMEM((rows // 2, width), bf16),
            pltpu.SemaphoreType.DMA((max(len(extras), 1),)),
        ]
        + [pltpu.SemaphoreType.DMA((TP_CHUNKS,))] * 6
        + swap_sems
        + [pltpu.SemaphoreType.DMA((count,))] * (2 * len(smalls))
        + line_scratch,
        compiler_params=pltpu.CompilerParams(
            collective_id=call_id, has_side_effects=True, vmem_limit_bytes=40 * 1024 * 1024
        ),
        cost_estimate=pl.CostEstimate(flops=0, bytes_accessed=0, transcendentals=0),
    )(part, *lines, *smalls, *[one[0] for one in swaps], *extras, *gains)


def fold(values):
    return values[:8] + values[8:]


def finish_middle(total, extras, gains, outs, place):
    middle = extras[0] + total
    outs[0][place] = middle
    outs[1][place] = (rms_parts(middle)[0] * gains[0]).astype(bf16)


def finish_grad_middle(total, extras, gains, outs, place):
    middle, cot = extras
    unit, inverse = rms_parts(middle)
    grad = cot + rms_back(total, gains[0], unit, inverse)
    outs[0][place] = grad
    outs[1][place] = grad.astype(bf16)
    outs[2][...] += fold(total * unit)


def finish_grad_tokens(total, extras, gains, outs, place):
    tokens, grad_middle = extras
    unit, inverse = rms_parts(tokens)
    outs[0][place] = (grad_middle + rms_back(total, gains[0], unit, inverse)).astype(bf16)
    outs[1][...] += fold(total * unit)


def finish_output(total, extras, gains, outs, place):
    outs[0][place] = (extras[0] + total).astype(bf16)


def by_parity(values, count, parity, axis):
    width = values.shape[axis] // count

    def chosen(which):
        return jnp.concatenate(
            [
                lax.slice_in_dim(values, at * width, (at + 1) * width, axis=axis)
                for at in range(which, count, 2)
            ],
            axis=axis,
        )

    even, odd = chosen(0), chosen(1)
    return jnp.where(parity == 0, even, odd), jnp.where(parity == 0, odd, even)


def tie(*values):
    return lax.optimization_barrier(values)


def line_sum(local, count):
    lines = [list(range(pair, count, 2)) for pair in range(2)]
    return lax.psum_scatter(local, "seq", scatter_dimension=0, tiled=True, axis_index_groups=lines)


def shards(
    count,
    tokens,
    doc_lengths,
    pad_mask,
    gain_mix,
    w_in,
    short_conv,
    pole_log_rate,
    residue,
    w_out,
    gain_ffn,
    w_gu,
    w_down,
    cotangent,
):
    rows, row_count, width = tokens.shape
    channels = w_in.shape[2]
    hidden_units = w_down.shape[0]
    poles = residue.shape[0]
    total_rows = rows * row_count
    me = lax.axis_index("seq")
    parity = lax.rem(me, 2)
    anchor = me * row_count
    places = anchor + jnp.arange(row_count)
    doc_ends = jnp.cumsum(doc_lengths, axis=1)
    begins = doc_ends - doc_lengths
    begin_tok = jax.vmap(doc_begin, in_axes=(None, 0))(places, begins)
    firsts = jnp.arange(count) * row_count
    begin_dev = jax.vmap(doc_begin, in_axes=(None, 0))(firsts, begins)
    begin_me = jax.vmap(doc_begin, in_axes=(None, 0))(anchor[None], begins)
    devices = jnp.arange(count)[None, :]
    earlier = devices < me
    carry_fwd = jnp.stack(
        [earlier & (begin_me < (devices + 1) * row_count), earlier & (devices >= 0) & (begin_me >= 0)],
        axis=1,
    )
    later = devices > me
    carry_bwd = jnp.stack(
        [later & (begin_dev < anchor + row_count), later & (begin_dev >= 0)], axis=1
    )
    carry_fwd = carry_fwd.reshape(2 * rows, count).astype(f32)
    carry_bwd = carry_bwd.reshape(2 * rows, count).astype(f32)
    masks = jnp.stack(
        [
            pad_mask != 0,
            begin_tok <= places[None, :] - 1,
            begin_tok <= places[None, :] - 2,
            places[None, :] >= begin_tok[:, -1:],
            begin_tok < anchor,
        ]
    ).astype(f32)
    masks = jnp.broadcast_to(masks[..., None], masks.shape + (128,))

    swap = [(i, i ^ 1) for i in range(count)]
    along = [(i, i + 1) for i in range(count - 1)]
    back = [(i + 1, i) for i in range(count - 1)]

    def partner(values):
        return lax.ppermute(values, "seq", swap)

    tail = lax.ppermute(tokens[:, -2:], "seq", along)
    tail = jnp.pad(tail, ((0, 0), (6, 0), (0, 0)))
    inputs_f = tokens.astype(f32)
    normed = (rms_parts(inputs_f)[0] * gain_mix).astype(bf16)
    normed_tail = (rms_parts(tail.astype(f32))[0] * gain_mix).astype(bf16)
    proj = jnp.einsum("btd,dkc->kbtc", normed, w_in, preferred_element_type=f32).astype(bf16)
    halo = jnp.einsum("btd,dkc->kbtc", normed_tail, w_in, preferred_element_type=f32).astype(bf16)

    conv_shape = (rows, row_count, channels)
    state_shape = (rows, poles, channels)
    pad_scratch = pltpu.VMEM((rows, row_count + 8, channels), f32)
    query, mixed, values, ends = vmem_call(
        conv_start_kernel,
        [(conv_shape, f32), ((2,) + conv_shape, f32), (conv_shape, f32), (state_shape, bf16)],
        [pad_scratch],
        (),
        proj,
        halo,
        short_conv,
        pole_log_rate,
        masks,
    )
    conv_out, gated, begin_state = vmem_call(
        conv_forward_kernel,
        [(conv_shape, f32), (conv_shape, bf16), (state_shape, f32)],
        [],
        (3,),
        values,
        query,
        spread(ends, count, 0),
        carry_fwd,
        pole_log_rate,
        residue,
        masks,
    )
    gated = gated.reshape(total_rows, channels)
    flat_tokens = tokens.reshape(total_rows, width)
    normed = normed.reshape(total_rows, width)
    cotangent = cotangent.reshape(total_rows, width)
    gain_mix = gain_mix.reshape(1, width)
    gain_ffn = gain_ffn.reshape(1, width)
    flat = (total_rows, width)

    def pair_up(own_send):
        return jnp.concatenate([own_send[0], partner(own_send[1])], axis=0)

    middle, normed_b, cot_pair, gated_pair = tp_sum(
        finish_middle,
        3,
        dot_nn(gated, w_out).astype(bf16),
        [flat_tokens],
        [gain_ffn],
        [(flat, f32), (flat, bf16)],
        (),
        [(cotangent, True), (gated, False)],
        count,
    )
    gate_up = jnp.einsum("td,dkf->ktf", normed_b, w_gu, preferred_element_type=f32)
    gate, up = gate_up[0], gate_up[1]
    grad_hidden = dot_nt(cotangent, w_down)
    sigmoid_g = jax.nn.sigmoid(gate)
    swish_out = gate * sigmoid_g
    hidden = (swish_out * up).astype(bf16)
    grad_gate = (grad_hidden * up * sigmoid_g * (1.0 + gate * (1.0 - sigmoid_g))).astype(bf16)
    grad_up = (grad_hidden * swish_out).astype(bf16)

    hidden_pair = jnp.concatenate([hidden, partner(hidden)], axis=0)
    part = jnp.einsum(
        "ktf,dkf->td", jnp.stack([grad_gate, grad_up]), w_gu, preferred_element_type=f32
    ).astype(bf16)
    down_local = dot_tn(cot_pair, hidden_pair).astype(bf16)
    out_part = dot_nn(hidden, w_down).astype(bf16)
    part, out_part = tie(part, out_part)
    part, down_local = tie(part, down_local)
    down_sum = line_sum(down_local, count)
    gate_pair = jnp.concatenate([grad_gate, partner(grad_gate)], axis=0)

    grad_middle, branch_grad, gain_ffn_sum, normed_b_pair = tp_sum(
        finish_grad_middle,
        4,
        part,
        [middle, cotangent],
        [gain_ffn],
        [(flat, f32), (flat, bf16), ((8, width), f32)],
        (2,),
        [(normed_b, True)],
        count,
    )
    branch_grad, normed_b_pair = tie(branch_grad, normed_b_pair)
    gate_local = dot_tn(normed_b_pair, gate_pair).astype(bf16)
    branch_grad, gate_local, grad_up = tie(branch_grad, gate_local, grad_up)
    gate_sum = line_sum(gate_local, count)
    up_other = partner(grad_up)
    grad_gated = dot_nt(branch_grad, w_out).astype(bf16).reshape(conv_shape)
    grad_conv, heads = vmem_call(
        conv_back_start_kernel,
        [(conv_shape, f32), (state_shape, bf16)],
        [],
        (),
        grad_gated,
        query,
        pole_log_rate,
        masks,
    )
    branch_own, branch_send = by_parity(branch_grad, count, parity, 1)
    heads, branch_send = tie(heads, branch_send)
    branch_other = partner(branch_send)
    all_heads = spread(heads, count, 1)
    up_local = dot_tn(normed_b_pair, jnp.concatenate([grad_up, up_other], axis=0)).astype(bf16)
    all_heads, up_local, down_sum = tie(all_heads, up_local, down_sum)
    up_sum = line_sum(up_local, count)
    grad_proj, front, grad_taps, grad_rate, grad_residue = vmem_call(
        conv_back_kernel,
        [
            ((3,) + conv_shape, f32),
            ((3, rows, 8, channels), f32),
            ((3, 3, channels), f32),
            ((poles, channels), f32),
            ((poles, channels), f32),
        ],
        [
            pltpu.VMEM((row_count, poles, channels), f32),
            pltpu.VMEM(conv_shape, f32),
            pad_scratch,
            pad_scratch,
        ],
        (10,),
        values,
        grad_conv,
        grad_gated,
        mixed,
        conv_out,
        proj,
        halo,
        short_conv,
        begin_state,
        all_heads,
        carry_bwd,
        pole_log_rate,
        residue,
        masks,
    )
    grad_proj, branch_other = tie(grad_proj, branch_other)
    returned = lax.ppermute(front[:, :, 6:], "seq", back)
    grad_proj = jnp.concatenate(
        [grad_proj[:, :, :-2], grad_proj[:, :, -2:] + returned], axis=2
    ).astype(bf16).reshape(3, total_rows, channels)
    part = jnp.einsum("ktc,dkc->td", grad_proj, w_in, preferred_element_type=f32).astype(bf16)
    part, gate_sum = tie(part, gate_sum)
    proj_other = partner(grad_proj)
    branch_pair = jnp.concatenate([branch_own, branch_other], axis=0)
    small = jnp.concatenate(
        [
            grad_rate,
            grad_residue,
            grad_taps.reshape(9, channels),
            jnp.sum(gain_ffn_sum, axis=0).reshape(-1, channels),
        ]
    )
    small = jnp.pad(small, ((0, (-small.shape[0]) % 16), (0, 0))).astype(bf16)
    grad_tokens, gain_mix_sum, normed_pair, small, grad_out = tp_sum(
        finish_grad_tokens,
        5,
        part,
        [flat_tokens, grad_middle],
        [gain_mix],
        [(flat, bf16), ((8, width), f32)],
        (1,),
        swaps=[(normed, True)],
        count=count,
        small=small,
        lines=[dot_tn(branch_pair, gated_pair).astype(bf16)],
    )
    in_local = [
        dot_tn(normed_pair, jnp.concatenate([grad_proj[k], proj_other[k]], axis=0)).astype(bf16)
        for k in range(3)
    ]
    grad_tokens, in_query, up_sum = tie(grad_tokens, in_local[0], up_sum)
    in_sum = line_sum(in_query, count)
    out_part, grad_tokens, in_query = tie(out_part, grad_tokens, in_query)

    gain_rows = width // channels
    gain_mix_sum = jnp.sum(gain_mix_sum, axis=0).reshape(-1, channels)
    gain_mix_sum = jnp.pad(gain_mix_sum, ((0, (-gain_rows) % 16), (0, 0))).astype(bf16)
    output, gathered, in_key, in_value = tp_sum(
        finish_output,
        6,
        out_part,
        [middle],
        [],
        [(flat, bf16)],
        count=count,
        small=gain_mix_sum,
        lines=in_local[1:],
    )
    small = jnp.sum(small.astype(f32), axis=0)
    grad_gain_mix = jnp.sum(gathered.astype(f32), axis=0)[:gain_rows].reshape(width)
    grad_down = down_sum.astype(f32).T
    grad_gu_w = jnp.stack([gate_sum.astype(f32), up_sum.astype(f32)], axis=1)
    grad_in = jnp.stack([in_sum.astype(f32), in_key, in_value]).transpose(1, 0, 2)

    taps_at = 2 * poles
    gain_at = taps_at + 9
    return (
        output.reshape(tokens.shape),
        grad_tokens.reshape(tokens.shape),
        grad_gain_mix,
        grad_in,
        small[taps_at:gain_at].reshape(3, 3, channels),
        small[:poles],
        small[poles:taps_at],
        grad_out.T,
        small[gain_at : gain_at + gain_rows].reshape(width),
        grad_gu_w,
        grad_down,
    )


def solution(mesh):
    in_specs = (
        P(None, "seq", None),
        P(),
        P(None, "seq"),
        P(),
        P(None, None, "tp"),
        P(None, None, "tp"),
        P(None, "tp"),
        P(None, "tp"),
        P("tp", None),
        P(),
        P(None, None, "tp"),
        P("tp", None),
        P(None, "seq", None),
    )
    out_specs = (
        P(None, "seq", None),
        P(None, "seq", None),
        P(),
        P("seq", None, "tp"),
        P(None, None, "tp"),
        P(None, "tp"),
        P(None, "tp"),
        P("tp", "seq"),
        P(),
        P("seq", None, "tp"),
        P("tp", "seq"),
    )
    return jax.shard_map(
        functools.partial(shards, mesh.shape["seq"]),
        mesh=mesh,
        in_specs=in_specs,
        out_specs=out_specs,
        check_vma=False,
    )
```

```python
import functools

import jax
import jax.numpy as jnp
from jax import lax
from jax.experimental import pallas as pl
from jax.experimental.pallas import tpu as pltpu
from jax.sharding import PartitionSpec as P

MESH = pl.DeviceIdType.MESH
epsilon = 1e-06
f32 = jnp.float32
bf16 = jnp.bfloat16
GROUP = 8
CHUNK = 32
TP_CHUNKS = 8


def doc_begin(places, begins):
    return jnp.max(jnp.where(begins[None, :] <= places[:, None], begins[None, :], 0), axis=1)


def rms_parts(values):
    inverse = lax.rsqrt(jnp.mean(values * values, axis=-1, keepdims=True) + epsilon)
    return (values * inverse, inverse)


def rms_back(grad_norm, gain_vec, unit_vec, inverse):
    scaled = grad_norm * gain_vec
    return inverse * (scaled - unit_vec * jnp.mean(scaled * unit_vec, axis=-1, keepdims=True))


def dot_nn(a, b):
    return lax.dot_general(a, b, (((1,), (0,)), ((), ())), preferred_element_type=f32)


def dot_nt(a, b):
    return lax.dot_general(a, b, (((1,), (1,)), ((), ())), preferred_element_type=f32)


def dot_tn(a, b):
    return lax.dot_general(a, b, (((0,), (0,)), ((), ())), preferred_element_type=f32)


def spread_kernel(count, own_ref, all_ref, send_sem, recv_sem, local_sem):
    me = lax.axis_index("seq")
    barrier = pltpu.get_barrier_semaphore()

    def greet(step, carry):
        pl.semaphore_signal(
            barrier, inc=1, device_id={"seq": lax.rem(me + step, count)}, device_id_type=MESH
        )
        return carry

    lax.fori_loop(1, count, greet, 0)
    pl.semaphore_wait(barrier, count - 1)
    local = pltpu.make_async_copy(own_ref, all_ref.at[me], local_sem)
    local.start()

    def copy(step, slot):
        return pltpu.make_async_remote_copy(
            src_ref=own_ref,
            dst_ref=all_ref.at[slot],
            send_sem=send_sem.at[step],
            recv_sem=recv_sem.at[step],
            device_id={"seq": lax.rem(me + step, count)},
            device_id_type=MESH,
        )

    def send(step, carry):
        copy(step, me).start()
        return carry

    lax.fori_loop(1, count, send, 0)
    local.wait()

    def finish(step, carry):
        arrived = copy(step, lax.rem(me + count - step, count))
        arrived.wait_send()
        arrived.wait_recv()
        return carry

    lax.fori_loop(1, count, finish, 0)


def spread(own, count, call_id):
    return pl.pallas_call(
        functools.partial(spread_kernel, count),
        out_shape=jax.ShapeDtypeStruct((count,) + own.shape, own.dtype),
        in_specs=[pl.BlockSpec(memory_space=pltpu.VMEM)],
        out_specs=pl.BlockSpec(memory_space=pltpu.VMEM),
        scratch_shapes=[
            pltpu.SemaphoreType.DMA((count,)),
            pltpu.SemaphoreType.DMA((count,)),
            pltpu.SemaphoreType.DMA,
        ],
        compiler_params=pltpu.CompilerParams(collective_id=call_id, has_side_effects=True),
    )(own)


def widen(mask, channels):
    return jnp.concatenate([mask] * (channels // mask.shape[-1]), axis=-1)


def conv_start_kernel(proj_ref, halo_ref, taps_ref, rate_ref, mask_ref, query_ref, mixed_ref, values_ref, end_ref, pad_ref):
    rows, tokens, channels = values_ref.shape
    poles = rate_ref.shape[0]
    for k in range(3):
        for row in range(rows):
            pad_ref[row, 0:8] = halo_ref[k, row].astype(f32)
            pad_ref[row, 8:] = proj_ref[k, row].astype(f32)
        for row in range(rows):
            for first in range(0, tokens, CHUNK):
                total = taps_ref[k, 0:1] * pad_ref[row, 8 + first : 8 + first + CHUNK]
                for tap in (1, 2):
                    allowed = widen(mask_ref[tap, row, first : first + CHUNK], channels)
                    begin = 8 - tap + first
                    total = total + taps_ref[k, tap : tap + 1] * pad_ref[row, begin : begin + CHUNK] * allowed
                if k == 0:
                    query_ref[row, first : first + CHUNK] = total
                else:
                    mixed_ref[k - 1, row, first : first + CHUNK] = total
                if k == 2:
                    keep = widen(mask_ref[0, row, first : first + CHUNK], channels)
                    product = mixed_ref[0, row, first : first + CHUNK] * total * keep
                    values_ref[row, first : first + CHUNK] = product.astype(bf16).astype(f32)
    decay = jnp.exp(-jnp.exp(rate_ref[...]))

    def step(group, states):
        for offset in range(GROUP):
            at = group * GROUP + offset
            states = tuple(
                states[row] * decay
                + values_ref[row, pl.ds(at, 1)] * widen(mask_ref[3, row, pl.ds(at, 1)], channels)
                for row in range(rows)
            )
        return states

    zero = jnp.zeros((poles, channels), f32)
    ends = lax.fori_loop(0, tokens // GROUP, step, (zero,) * rows)
    for row in range(rows):
        end_ref[row] = ends[row].astype(bf16)


def carried_state(all_ref, carry_ref, row, order, decay_far, shape):
    state = jnp.zeros(shape, f32)
    for position in order:
        advance = carry_ref[2 * row + 1, position]
        state = state * (1.0 + advance * (decay_far - 1.0)) + all_ref[position, row].astype(f32) * carry_ref[2 * row, position]
    return state


def conv_forward_kernel(values_ref, query_ref, all_ref, carry_ref, rate_ref, residue_ref, mask_ref, conv_ref, gated_ref, begin_ref):
    rows, tokens, channels = values_ref.shape
    poles = rate_ref.shape[0]
    rate = jnp.exp(rate_ref[...])
    decay = jnp.exp(-rate)
    decay_far = jnp.exp(-rate * float(tokens))
    weight = residue_ref[...] * jnp.sqrt(rate)
    starts = []
    for row in range(rows):
        start = carried_state(all_ref, carry_ref, row, range(all_ref.shape[0]), decay_far, (poles, channels))
        begin_ref[row] = start
        starts.append(start)

    def step(group, states):
        for offset in range(GROUP):
            at = group * GROUP + offset
            following = []
            for row in range(rows):
                same = widen(mask_ref[1, row, pl.ds(at, 1)], channels)
                state = states[row] * (decay * same) + values_ref[row, pl.ds(at, 1)]
                conv_ref[row, pl.ds(at, 1)] = jnp.sum(state * weight, axis=0, keepdims=True)
                following.append(state)
            states = tuple(following)
        return states

    lax.fori_loop(0, tokens // GROUP, step, tuple(starts))
    for row in range(rows):
        for first in range(0, tokens, CHUNK):
            part = slice(first, first + CHUNK)
            gated_ref[row, part] = (query_ref[row, part] * conv_ref[row, part]).astype(bf16)


def conv_back_start_kernel(grad_gated_ref, query_ref, rate_ref, mask_ref, grad_conv_ref, head_ref):
    rows, tokens, channels = query_ref.shape
    poles = rate_ref.shape[0]
    for row in range(rows):
        for first in range(0, tokens, CHUNK):
            part = slice(first, first + CHUNK)
            product = grad_gated_ref[row, part].astype(f32) * query_ref[row, part]
            grad_conv_ref[row, part] = product.astype(bf16).astype(f32)
    decay = jnp.exp(-jnp.exp(rate_ref[...]))

    def step(group, states):
        for offset in range(GROUP):
            at = tokens - 1 - (group * GROUP + offset)
            states = tuple(
                states[row] * decay
                + grad_conv_ref[row, pl.ds(at, 1)] * widen(mask_ref[4, row, pl.ds(at, 1)], channels)
                for row in range(rows)
            )
        return states

    zero = jnp.zeros((poles, channels), f32)
    heads = lax.fori_loop(0, tokens // GROUP, step, (zero,) * rows)
    for row in range(rows):
        head_ref[row] = heads[row].astype(bf16)


def conv_back_kernel(
    values_ref,
    grad_conv_ref,
    grad_gated_ref,
    mixed_ref,
    conv_ref,
    proj_ref,
    halo_ref,
    taps_ref,
    begin_ref,
    all_ref,
    carry_ref,
    rate_ref,
    residue_ref,
    mask_ref,
    grad_proj_ref,
    front_ref,
    grad_taps_ref,
    grad_rate_ref,
    grad_residue_ref,
    history_ref,
    grad_values_ref,
    pad_ref,
    padded_ref,
):
    rows, tokens, channels = values_ref.shape
    poles = rate_ref.shape[0]
    count = all_ref.shape[0]
    rate = jnp.exp(rate_ref[...])
    decay = jnp.exp(-rate)
    decay_far = jnp.exp(-rate * float(tokens))
    root = jnp.sqrt(rate)
    weight = residue_ref[...] * root
    shape = (poles, channels)
    zero = jnp.zeros(shape, f32)
    grad_residue_ref[...] = zero
    grad_rate_ref[...] = zero
    for row in range(rows):

        def ahead(group, carry):
            state, total = carry
            for offset in range(GROUP):
                at = group * GROUP + offset
                same = widen(mask_ref[1, row, pl.ds(at, 1)], channels)
                history_ref[at] = state
                state = state * (decay * same) + values_ref[row, pl.ds(at, 1)]
                total = total + state * grad_conv_ref[row, pl.ds(at, 1)]
            return state, total

        total = lax.fori_loop(0, tokens // GROUP, ahead, (begin_ref[row], zero))[1]

        def behind(group, carry):
            incoming, cross = carry
            for offset in range(GROUP):
                at = tokens - 1 - (group * GROUP + offset)
                same = widen(mask_ref[1, row, pl.ds(at, 1)], channels)
                state = incoming + grad_conv_ref[row, pl.ds(at, 1)]
                grad_values_ref[row, pl.ds(at, 1)] = jnp.sum(state * weight, axis=0, keepdims=True)
                incoming = state * (decay * same)
                cross = cross + incoming * history_ref[at]
            return incoming, cross

        start = carried_state(all_ref, carry_ref, row, range(count - 1, -1, -1), decay_far, shape)
        cross = lax.fori_loop(0, tokens // GROUP, behind, (start * decay, zero))[1]
        grad_residue_ref[...] += root * total
        grad_rate_ref[...] += weight * (0.5 * total - rate * cross)

    for k in range(3):
        for row in range(rows):
            pad_ref[row, 0:8] = halo_ref[k, row].astype(f32)
            pad_ref[row, 8:] = proj_ref[k, row].astype(f32)
            padded_ref[row, 0:8] = jnp.zeros((8, channels), f32)
        sums = [jnp.zeros((1, channels), f32) for tap in range(3)]
        for row in range(rows):
            for first in range(0, tokens, CHUNK):
                part = slice(first, first + CHUNK)
                if k == 0:
                    grad_mixed = grad_gated_ref[row, part].astype(f32) * conv_ref[row, part]
                else:
                    keep = widen(mask_ref[0, row, part], channels)
                    grad_mixed = grad_values_ref[row, part] * mixed_ref[2 - k, row, part] * keep
                padded_ref[row, 8 + first : 8 + first + CHUNK] = taps_ref[k, 0:1] * grad_mixed
                sums[0] = sums[0] + jnp.sum(
                    grad_mixed * pad_ref[row, 8 + first : 8 + first + CHUNK], axis=0, keepdims=True
                )
                for tap in (1, 2):
                    begin = 8 - tap + first
                    allowed = grad_mixed * widen(mask_ref[tap, row, part], channels)
                    padded_ref[row, begin : begin + CHUNK] += taps_ref[k, tap : tap + 1] * allowed
                    sums[tap] = sums[tap] + jnp.sum(
                        allowed * pad_ref[row, begin : begin + CHUNK], axis=0, keepdims=True
                    )
            grad_proj_ref[k, row] = padded_ref[row, 8:]
            front_ref[k, row] = padded_ref[row, 0:8]
        for tap in range(3):
            grad_taps_ref[k, tap : tap + 1] = sums[tap]


def vmem_call(kernel, outs, scratch, smem_at, *operands):
    specs = [
        pl.BlockSpec(memory_space=pltpu.SMEM if at in smem_at else pltpu.VMEM)
        for at in range(len(operands))
    ]
    return pl.pallas_call(
        kernel,
        out_shape=[jax.ShapeDtypeStruct(shape, kind) for shape, kind in outs],
        in_specs=specs,
        out_specs=[pl.BlockSpec(memory_space=pltpu.VMEM)] * len(outs),
        scratch_shapes=scratch,
        compiler_params=pltpu.CompilerParams(vmem_limit_bytes=48 * 1024 * 1024),
    )(*operands)


def tp_sum_kernel(finish, extras, gains, outs, zeroed, swaps, count, small, lines, part_ref, *refs):
    line_refs, refs = refs[:lines], refs[lines:]
    pair_count = sum(swaps)
    if small:
        small_ref, refs = refs[0], refs[1:]
    swap_refs, refs = refs[: len(swaps)], refs[len(swaps) :]
    far_refs = refs[:extras]
    gain_refs = refs[extras : extras + gains]
    out_refs = refs[extras + gains : extras + gains + outs]
    pair_refs = refs[extras + gains + outs : extras + gains + outs + pair_count]
    scratch = refs[extras + gains + outs + pair_count :]
    if small:
        all_ref, scratch = scratch[0], scratch[1:]
    line_outs, scratch = scratch[:lines], scratch[lines:]
    if lines:
        (line_acc, line_got, line_sent, line_came), scratch = scratch[-4:], scratch[:-4]
    if small:
        scratch, spread_sems = scratch[:-2], scratch[-2:]
    near_refs, scratch = scratch[:extras], scratch[extras:]
    total_ref, recv_a, half_ref, recv_b, load_sem, sent_a, got_a, sent_b, got_b, sent_c, got_c, *swap_sems = scratch
    rows = part_ref.shape[0]
    half = rows // 2
    chunk = half // TP_CHUNKS
    me = lax.axis_index("tp")
    core = lax.rem(me, 2)
    near = me + 1 - 2 * core
    far = lax.rem(me + 2, 4)
    own = core * half
    other = half - own
    for at in zeroed:
        out_refs[at][...] = jnp.zeros(out_refs[at].shape, out_refs[at].dtype)
    loads = [
        pltpu.make_async_copy(source, target, load_sem.at[at])
        for at, (source, target) in enumerate(zip(far_refs, near_refs))
    ]
    for load in loads:
        load.start()
    place_seq = lax.axis_index("seq")
    parity = lax.rem(place_seq, 2)
    mate = place_seq + 1 - 2 * parity
    keeps, exchanges, forwards = [], [], []
    sources = []
    for source, stacked in zip(swap_refs, swaps):
        sources += [source] if stacked == 1 else [source.at[at] for at in range(stacked)]
    for at, (source, target) in enumerate(zip(sources, pair_refs)):
        height, extent = source.shape
        sliced = target.shape[1] < extent
        lower, upper = pl.ds(0, height), pl.ds(height, height)
        if not sliced:
            keeps.append(pltpu.make_async_copy(source, target.at[lower], swap_sems[0].at[at, 0]))
            exchanges.append(
                pltpu.make_async_remote_copy(
                    src_ref=source,
                    dst_ref=target.at[upper],
                    send_sem=swap_sems[1].at[at, 0],
                    recv_sem=swap_sems[2].at[at, 0],
                    device_id={"seq": mate},
                    device_id_type=MESH,
                )
            )
            continue
        wide = extent // count
        half_pieces = count // 4

        def columns(which):
            return pl.ds(pl.multiple_of(which * wide, wide), wide)

        for piece in range(2 * half_pieces):
            keeps.append(
                pltpu.make_async_copy(
                    source.at[:, columns(2 * piece + parity)],
                    target.at[lower, pl.ds(piece * wide, wide)],
                    swap_sems[0].at[at, piece],
                )
            )
        for piece in range(half_pieces):
            mine = core * half_pieces + piece
            theirs = half_pieces - core * half_pieces + piece
            exchanges.append(
                pltpu.make_async_remote_copy(
                    src_ref=source.at[:, columns(2 * mine + 1 - parity)],
                    dst_ref=target.at[upper, columns(mine)],
                    send_sem=swap_sems[1].at[at, piece],
                    recv_sem=swap_sems[2].at[at, piece],
                    device_id={"seq": mate},
                    device_id_type=MESH,
                )
            )

            def hand_on(which, at=at, piece=piece, target=target, upper=upper, columns=columns):
                return pltpu.make_async_remote_copy(
                    src_ref=target.at[upper, columns(which)],
                    dst_ref=target.at[upper, columns(which)],
                    send_sem=swap_sems[3].at[at, piece],
                    recv_sem=swap_sems[4].at[at, piece],
                    device_id={"tp": near},
                    device_id_type=MESH,
                )

            forwards.append((exchanges[-1], hand_on(mine), hand_on(theirs)))
    barrier = pltpu.get_barrier_semaphore()
    for device in (near, far):
        pl.semaphore_signal(barrier, inc=1, device_id={"tp": device}, device_id_type=MESH)
    if swaps:
        pl.semaphore_signal(barrier, inc=1, device_id={"seq": mate}, device_id_type=MESH)
    if lines and not small:
        for offset in (2, count - 2):
            device = lax.rem(place_seq + offset, count)
            pl.semaphore_signal(barrier, inc=1, device_id={"seq": device}, device_id_type=MESH)
    if small:

        def greet(step, carry):
            device = lax.rem(place_seq + step, count)
            pl.semaphore_signal(barrier, inc=1, device_id={"seq": device}, device_id_type=MESH)
            return carry

        lax.fori_loop(1, count, greet, 0)
    greeted = count - 1 if small else 2 if lines else 0
    pl.semaphore_wait(barrier, 2 + (1 if swaps else 0) + greeted)

    def spread_copy(step, slot):
        return pltpu.make_async_remote_copy(
            src_ref=small_ref,
            dst_ref=all_ref.at[slot],
            send_sem=spread_sems[0].at[step],
            recv_sem=spread_sems[1].at[step],
            device_id={"seq": lax.rem(place_seq + step, count)},
            device_id_type=MESH,
        )


    size = count // 2
    spot = place_seq // 2

    def along(way):
        return spot if way == 0 else size - 1 - spot

    def line_piece(unit, which):
        height = line_refs[unit].shape[0] // size
        return line_refs[unit].at[pl.ds(pl.multiple_of(which * height, height), height)]

    def line_copy(unit, way, step):
        source = line_piece(unit, (1 - way) * (size - 1)) if step == 1 else line_acc.at[unit, way, step - 2]
        return pltpu.make_async_remote_copy(
            src_ref=source,
            dst_ref=line_got.at[unit, way, step - 1],
            send_sem=line_sent.at[unit, way, step - 1],
            recv_sem=line_came.at[unit, way, step - 1],
            device_id={"seq": lax.rem(place_seq + (2, count - 2)[way], count)},
            device_id_type=MESH,
        )

    def sends(way, step):
        return along(way) <= min(step - 1, size - 2)

    def takes(way, step):
        return jnp.logical_and(along(way) >= 1, along(way) <= step)

    def line_send(step):
        for unit in range(lines):
            for way in range(2):

                @pl.when(sends(way, step))
                def _(unit=unit, way=way):
                    line_copy(unit, way, step).start()

    def line_take(step):
        for unit in range(lines):
            for way in range(2):

                @pl.when(takes(way, step))
                def _(unit=unit, way=way):
                    line_copy(unit, way, step).wait_recv()

                if step < size - 1:
                    ahead = (size - step - 1, step + 1)[way]
                    piece = line_piece(unit, lax.rem(spot + ahead, size))

                    @pl.when(takes(way, step))
                    def _(unit=unit, way=way, piece=piece):
                        added = line_got[unit, way, step - 1].astype(f32) + piece[...].astype(f32)
                        line_acc[unit, way, step - 1] = added.astype(bf16)

                    @pl.when(along(way) == 0)
                    def _(unit=unit, way=way, piece=piece):
                        line_acc[unit, way, step - 1] = piece[...]

    def line_advance(step):
        if lines and step < size - 1:
            line_take(step)
            line_send(step + 1)

    def span(base, at, size=chunk):
        return pl.ds(pl.multiple_of(base + at * size, size), size)

    def first(at, source):
        return pltpu.make_async_remote_copy(
            src_ref=part_ref.at[span(source, at)],
            dst_ref=recv_a.at[span(0, at)],
            send_sem=sent_a.at[at],
            recv_sem=got_a.at[at],
            device_id={"tp": near},
            device_id_type=MESH,
        )

    def second(at):
        return pltpu.make_async_remote_copy(
            src_ref=half_ref.at[span(0, at)],
            dst_ref=recv_b.at[span(0, at)],
            send_sem=sent_b.at[at],
            recv_sem=got_b.at[at],
            device_id={"tp": far},
            device_id_type=MESH,
        )

    def third(at, base):
        return pltpu.make_async_remote_copy(
            src_ref=total_ref.at[span(base, at)],
            dst_ref=total_ref.at[span(base, at)],
            send_sem=sent_c.at[at],
            recv_sem=got_c.at[at],
            device_id={"tp": near},
            device_id_type=MESH,
        )

    def apply(base, at):
        for inner in range(chunk // 16):
            place = pl.ds(pl.multiple_of(base + at * chunk + inner * 16, 16), 16)
            finish(
                total_ref[place].astype(f32),
                [ref[place].astype(f32) for ref in near_refs],
                [ref[...] for ref in gain_refs],
                out_refs,
                place,
            )

    def send_first(at, carry):
        first(at, other).start()
        return carry

    lax.fori_loop(0, TP_CHUNKS, send_first, 0)
    if lines and size > 1:
        line_send(1)

    def send_second(at, carry):
        first(at, other).wait_recv()
        summed = part_ref[span(own, at)].astype(f32) + recv_a[span(0, at)].astype(f32)
        half_ref[span(0, at)] = summed.astype(bf16)
        second(at).start()
        return carry

    lax.fori_loop(0, TP_CHUNKS, send_second, 0)
    for copy in exchanges + keeps:
        copy.start()
    if small:

        def send_small(step, carry):
            spread_copy(step, place_seq).start()
            return carry

        lax.fori_loop(1, count, send_small, 0)
        all_ref[place_seq] = small_ref[...]
    line_advance(1)
    for load in loads:
        load.wait()

    def send_third(at, carry):
        second(at).wait_recv()
        summed = half_ref[span(0, at)].astype(f32) + recv_b[span(0, at)].astype(f32)
        total_ref[span(own, at)] = summed.astype(bf16)
        third(at, own).start()
        apply(own, at)
        return carry

    lax.fori_loop(0, TP_CHUNKS // 2, send_third, 0)
    line_advance(2)
    lax.fori_loop(TP_CHUNKS // 2, TP_CHUNKS, send_third, 0)
    for exchange, onward, _ in forwards:
        exchange.wait_recv()
        onward.start()

    def take_third(at, carry):
        third(at, other).wait_recv()
        apply(other, at)
        return carry

    lax.fori_loop(0, TP_CHUNKS, take_third, 0)

    for step in range(3, size - 1):
        line_advance(step)
    if lines and size > 1:
        line_take(size - 1)
    for unit in range(lines):
        line_outs[unit][...] = line_piece(unit, spot)[...].astype(f32)
        for way in range(2 if size > 1 else 0):

            @pl.when(along(way) >= 1)
            def _(unit=unit, way=way):
                line_outs[unit][...] += line_got[unit, way, size - 2].astype(f32)

            for step in range(1, size):

                @pl.when(sends(way, step))
                def _(unit=unit, way=way, step=step):
                    line_copy(unit, way, step).wait_send()

    def drain(at, carry):
        first(at, other).wait_send()
        second(at).wait_send()
        third(at, own).wait_send()
        return carry

    lax.fori_loop(0, TP_CHUNKS, drain, 0)
    for copy in keeps:
        copy.wait()
    handed = [id(exchange) for exchange, _, _ in forwards]
    for copy in exchanges:
        copy.wait_send()
        if id(copy) not in handed:
            copy.wait_recv()
    for _, onward, inward in forwards:
        onward.wait_send()
        inward.wait_recv()
    if small:

        def finish_small(step, carry):
            arrived = spread_copy(step, lax.rem(place_seq + count - step, count))
            arrived.wait_send()
            arrived.wait_recv()
            return carry

        lax.fori_loop(1, count, finish_small, 0)


def tp_sum(finish, call_id, part, extras, gains, outs, zeroed=(), swaps=(), count=2, small=None, lines=()):
    rows, width = part.shape
    vmem = pl.BlockSpec(memory_space=pltpu.VMEM)
    anywhere = pl.BlockSpec(memory_space=pl.ANY)
    parity = lax.rem(lax.axis_index("seq"), 2)
    if any(one[1] and (count % 4 or one[0].shape[1] // count % 128) for one in swaps):
        swap = [(i, i ^ 1) for i in range(count)]
        after = []
        for array, sliced in swaps:
            own, send = by_parity(array, count, parity, 1) if sliced else (array, array)
            after.append(jnp.concatenate([own, lax.ppermute(send, "seq", swap)], axis=0))
        results = tp_sum(
            finish, call_id, part, extras, gains, outs, zeroed, (), count, small, lines
        )
        return [*results[: len(outs)], *after, *results[len(outs) :]]
    pairs, stacked = [], []
    for array, sliced in swaps:
        height, extent = array.shape[-2:]
        stacked.append(array.shape[0] if array.ndim == 3 else 1)
        pair = jax.ShapeDtypeStruct((2 * height, extent // (2 if sliced else 1)), array.dtype)
        pairs += [pair] * stacked[-1]
    swap_sems = [pltpu.SemaphoreType.DMA((len(pairs), max(count // 2, 1)))] * 5 if swaps else []
    smalls = [] if small is None else [small]
    slots = max(count // 2 - 1, 1)
    summed, line_scratch = [], []
    if lines:
        height, extent = lines[0].shape
        height = height // (count // 2)
        summed = [jax.ShapeDtypeStruct((height, extent), f32)] * len(lines)
        line_scratch = [pltpu.VMEM((len(lines), 2, slots, height, extent), bf16)] * 2
        line_scratch = line_scratch + [pltpu.SemaphoreType.DMA((len(lines), 2, slots))] * 2
    gathered = [jax.ShapeDtypeStruct((count,) + one.shape, one.dtype) for one in smalls]
    return pl.pallas_call(
        functools.partial(tp_sum_kernel, finish, len(extras), len(gains), len(outs), zeroed, tuple(stacked), count, bool(smalls), len(lines)),
        out_shape=[jax.ShapeDtypeStruct(shape, kind) for shape, kind in outs] + pairs + gathered + summed,
        in_specs=[vmem] * (1 + len(lines) + len(smalls)) + [anywhere] * (len(swaps) + len(extras)) + [vmem] * len(gains),
        out_specs=[vmem] * len(outs) + [anywhere] * len(pairs) + [vmem] * (len(smalls) + len(lines)),
        scratch_shapes=[pltpu.VMEM(extra.shape, extra.dtype) for extra in extras]
        + [
            pltpu.VMEM((rows, width), bf16),
            pltpu.VMEM((rows // 2, width), bf16),
            pltpu.VMEM((rows // 2, width), bf16),
            pltpu.VMEM((rows // 2, width), bf16),
            pltpu.SemaphoreType.DMA((max(len(extras), 1),)),
        ]
        + [pltpu.SemaphoreType.DMA((TP_CHUNKS,))] * 6
        + swap_sems
        + [pltpu.SemaphoreType.DMA((count,))] * (2 * len(smalls))
        + line_scratch,
        compiler_params=pltpu.CompilerParams(
            collective_id=call_id, has_side_effects=True, vmem_limit_bytes=40 * 1024 * 1024
        ),
        cost_estimate=pl.CostEstimate(flops=0, bytes_accessed=0, transcendentals=0),
    )(part, *lines, *smalls, *[one[0] for one in swaps], *extras, *gains)


def fold(values):
    return values[:8] + values[8:]


def finish_middle(total, extras, gains, outs, place):
    middle = extras[0] + total
    outs[0][place] = middle
    outs[1][place] = (rms_parts(middle)[0] * gains[0]).astype(bf16)


def finish_grad_middle(total, extras, gains, outs, place):
    middle, cot = extras
    unit, inverse = rms_parts(middle)
    grad = cot + rms_back(total, gains[0], unit, inverse)
    outs[0][place] = grad
    outs[1][place] = grad.astype(bf16)
    outs[2][...] += fold(total * unit)


def finish_grad_tokens(total, extras, gains, outs, place):
    tokens, grad_middle = extras
    unit, inverse = rms_parts(tokens)
    outs[0][place] = (grad_middle + rms_back(total, gains[0], unit, inverse)).astype(bf16)
    outs[1][...] += fold(total * unit)


def finish_output(total, extras, gains, outs, place):
    outs[0][place] = (extras[0] + total).astype(bf16)


def by_parity(values, count, parity, axis):
    width = values.shape[axis] // count

    def chosen(which):
        return jnp.concatenate(
            [
                lax.slice_in_dim(values, at * width, (at + 1) * width, axis=axis)
                for at in range(which, count, 2)
            ],
            axis=axis,
        )

    even, odd = chosen(0), chosen(1)
    return jnp.where(parity == 0, even, odd), jnp.where(parity == 0, odd, even)


def tie(*values):
    return lax.optimization_barrier(values)


def line_sum(local, count):
    lines = [list(range(pair, count, 2)) for pair in range(2)]
    return lax.psum_scatter(local, "seq", scatter_dimension=0, tiled=True, axis_index_groups=lines)


def shards(
    count,
    tokens,
    doc_lengths,
    pad_mask,
    gain_mix,
    w_in,
    short_conv,
    pole_log_rate,
    residue,
    w_out,
    gain_ffn,
    w_gu,
    w_down,
    cotangent,
):
    rows, row_count, width = tokens.shape
    channels = w_in.shape[2]
    hidden_units = w_down.shape[0]
    poles = residue.shape[0]
    total_rows = rows * row_count
    me = lax.axis_index("seq")
    parity = lax.rem(me, 2)
    anchor = me * row_count
    places = anchor + jnp.arange(row_count)
    doc_ends = jnp.cumsum(doc_lengths, axis=1)
    begins = doc_ends - doc_lengths
    begin_tok = jax.vmap(doc_begin, in_axes=(None, 0))(places, begins)
    firsts = jnp.arange(count) * row_count
    begin_dev = jax.vmap(doc_begin, in_axes=(None, 0))(firsts, begins)
    begin_me = jax.vmap(doc_begin, in_axes=(None, 0))(anchor[None], begins)
    devices = jnp.arange(count)[None, :]
    earlier = devices < me
    carry_fwd = jnp.stack(
        [earlier & (begin_me < (devices + 1) * row_count), earlier & (devices >= 0) & (begin_me >= 0)],
        axis=1,
    )
    later = devices > me
    carry_bwd = jnp.stack(
        [later & (begin_dev < anchor + row_count), later & (begin_dev >= 0)], axis=1
    )
    carry_fwd = carry_fwd.reshape(2 * rows, count).astype(f32)
    carry_bwd = carry_bwd.reshape(2 * rows, count).astype(f32)
    masks = jnp.stack(
        [
            pad_mask != 0,
            begin_tok <= places[None, :] - 1,
            begin_tok <= places[None, :] - 2,
            places[None, :] >= begin_tok[:, -1:],
            begin_tok < anchor,
        ]
    ).astype(f32)
    masks = jnp.broadcast_to(masks[..., None], masks.shape + (128,))

    swap = [(i, i ^ 1) for i in range(count)]
    along = [(i, i + 1) for i in range(count - 1)]
    back = [(i + 1, i) for i in range(count - 1)]

    def partner(values):
        return lax.ppermute(values, "seq", swap)

    tail = lax.ppermute(tokens[:, -2:], "seq", along)
    tail = jnp.pad(tail, ((0, 0), (6, 0), (0, 0)))
    inputs_f = tokens.astype(f32)
    normed = (rms_parts(inputs_f)[0] * gain_mix).astype(bf16)
    normed_tail = (rms_parts(tail.astype(f32))[0] * gain_mix).astype(bf16)
    proj = jnp.einsum("btd,dkc->kbtc", normed, w_in, preferred_element_type=f32).astype(bf16)
    halo = jnp.einsum("btd,dkc->kbtc", normed_tail, w_in, preferred_element_type=f32).astype(bf16)

    conv_shape = (rows, row_count, channels)
    state_shape = (rows, poles, channels)
    pad_scratch = pltpu.VMEM((rows, row_count + 8, channels), f32)
    query, mixed, values, ends = vmem_call(
        conv_start_kernel,
        [(conv_shape, f32), ((2,) + conv_shape, f32), (conv_shape, f32), (state_shape, bf16)],
        [pad_scratch],
        (),
        proj,
        halo,
        short_conv,
        pole_log_rate,
        masks,
    )
    conv_out, gated, begin_state = vmem_call(
        conv_forward_kernel,
        [(conv_shape, f32), (conv_shape, bf16), (state_shape, f32)],
        [],
        (3,),
        values,
        query,
        spread(ends, count, 0),
        carry_fwd,
        pole_log_rate,
        residue,
        masks,
    )
    gated = gated.reshape(total_rows, channels)
    flat_tokens = tokens.reshape(total_rows, width)
    normed = normed.reshape(total_rows, width)
    cotangent = cotangent.reshape(total_rows, width)
    gain_mix = gain_mix.reshape(1, width)
    gain_ffn = gain_ffn.reshape(1, width)
    flat = (total_rows, width)

    def pair_up(own_send):
        return jnp.concatenate([own_send[0], partner(own_send[1])], axis=0)

    middle, normed_b, cot_pair, gated_pair = tp_sum(
        finish_middle,
        3,
        dot_nn(gated, w_out).astype(bf16),
        [flat_tokens],
        [gain_ffn],
        [(flat, f32), (flat, bf16)],
        (),
        [(cotangent, True), (gated, False)],
        count,
    )
    gate_up = jnp.einsum("td,dkf->ktf", normed_b, w_gu, preferred_element_type=f32)
    gate, up = gate_up[0], gate_up[1]
    grad_hidden = dot_nt(cotangent, w_down)
    sigmoid_g = jax.nn.sigmoid(gate)
    swish_out = gate * sigmoid_g
    hidden = (swish_out * up).astype(bf16)
    grad_gate = (grad_hidden * up * sigmoid_g * (1.0 + gate * (1.0 - sigmoid_g))).astype(bf16)
    grad_up = (grad_hidden * swish_out).astype(bf16)

    hidden_pair = jnp.concatenate([hidden, partner(hidden)], axis=0)
    part = jnp.einsum(
        "ktf,dkf->td", jnp.stack([grad_gate, grad_up]), w_gu, preferred_element_type=f32
    ).astype(bf16)
    down_local = dot_tn(cot_pair, hidden_pair).astype(bf16)
    out_part = dot_nn(hidden, w_down).astype(bf16)
    part, out_part = tie(part, out_part)
    part, down_local = tie(part, down_local)
    down_sum = line_sum(down_local, count)
    gate_pair = jnp.concatenate([grad_gate, partner(grad_gate)], axis=0)

    grad_middle, branch_grad, gain_ffn_sum, normed_b_pair = tp_sum(
        finish_grad_middle,
        4,
        part,
        [middle, cotangent],
        [gain_ffn],
        [(flat, f32), (flat, bf16), ((8, width), f32)],
        (2,),
        [(normed_b, True)],
        count,
    )
    branch_grad, normed_b_pair = tie(branch_grad, normed_b_pair)
    gate_local = dot_tn(normed_b_pair, gate_pair).astype(bf16)
    branch_grad, gate_local = tie(branch_grad, gate_local)
    gate_sum = line_sum(gate_local, count)
    grad_gated = dot_nt(branch_grad, w_out).astype(bf16).reshape(conv_shape)
    grad_conv, heads = vmem_call(
        conv_back_start_kernel,
        [(conv_shape, f32), (state_shape, bf16)],
        [],
        (),
        grad_gated,
        query,
        pole_log_rate,
        masks,
    )
    branch_own, branch_send = by_parity(branch_grad, count, parity, 1)
    heads, branch_send = tie(heads, branch_send)
    branch_other = partner(branch_send)
    all_heads = spread(heads, count, 1)
    all_heads, grad_up, branch_other = tie(all_heads, grad_up, branch_other)
    up_other = partner(grad_up)
    grad_proj, front, grad_taps, grad_rate, grad_residue = vmem_call(
        conv_back_kernel,
        [
            ((3,) + conv_shape, f32),
            ((3, rows, 8, channels), f32),
            ((3, 3, channels), f32),
            ((poles, channels), f32),
            ((poles, channels), f32),
        ],
        [
            pltpu.VMEM((row_count, poles, channels), f32),
            pltpu.VMEM(conv_shape, f32),
            pad_scratch,
            pad_scratch,
        ],
        (10,),
        values,
        grad_conv,
        grad_gated,
        mixed,
        conv_out,
        proj,
        halo,
        short_conv,
        begin_state,
        all_heads,
        carry_bwd,
        pole_log_rate,
        residue,
        masks,
    )
    grad_proj, normed_b_pair, down_sum = tie(grad_proj, normed_b_pair, down_sum)
    returned = lax.ppermute(front[:, :, 6:], "seq", back)
    up_local = dot_tn(normed_b_pair, jnp.concatenate([grad_up, up_other], axis=0)).astype(bf16)
    returned, up_local = tie(returned, up_local)
    up_sum = line_sum(up_local, count)
    grad_proj = jnp.concatenate(
        [grad_proj[:, :, :-2], grad_proj[:, :, -2:] + returned], axis=2
    ).astype(bf16).reshape(3, total_rows, channels)
    part = jnp.einsum("ktc,dkc->td", grad_proj, w_in, preferred_element_type=f32).astype(bf16)
    part, gate_sum = tie(part, gate_sum)
    proj_other = partner(grad_proj)
    branch_pair = jnp.concatenate([branch_own, branch_other], axis=0)
    small = jnp.concatenate(
        [
            grad_rate,
            grad_residue,
            grad_taps.reshape(9, channels),
            jnp.sum(gain_ffn_sum, axis=0).reshape(-1, channels),
        ]
    )
    small = jnp.pad(small, ((0, (-small.shape[0]) % 16), (0, 0))).astype(bf16)
    grad_tokens, gain_mix_sum, normed_pair, small, grad_out = tp_sum(
        finish_grad_tokens,
        5,
        part,
        [flat_tokens, grad_middle],
        [gain_mix],
        [(flat, bf16), ((8, width), f32)],
        (1,),
        swaps=[(normed, True)],
        count=count,
        small=small,
        lines=[dot_tn(branch_pair, gated_pair).astype(bf16)],
    )
    in_local = [
        dot_tn(normed_pair, jnp.concatenate([grad_proj[k], proj_other[k]], axis=0)).astype(bf16)
        for k in range(3)
    ]
    grad_tokens, in_query, up_sum = tie(grad_tokens, in_local[0], up_sum)
    in_sum = line_sum(in_query, count)
    out_part, grad_tokens, in_query = tie(out_part, grad_tokens, in_query)

    gain_rows = width // channels
    gain_mix_sum = jnp.sum(gain_mix_sum, axis=0).reshape(-1, channels)
    gain_mix_sum = jnp.pad(gain_mix_sum, ((0, (-gain_rows) % 16), (0, 0))).astype(bf16)
    output, gathered, in_key, in_value = tp_sum(
        finish_output,
        6,
        out_part,
        [middle],
        [],
        [(flat, bf16)],
        count=count,
        small=gain_mix_sum,
        lines=in_local[1:],
    )
    small = jnp.sum(small.astype(f32), axis=0)
    grad_gain_mix = jnp.sum(gathered.astype(f32), axis=0)[:gain_rows].reshape(width)
    grad_down = down_sum.astype(f32).T
    grad_gu_w = jnp.stack([gate_sum.astype(f32), up_sum.astype(f32)], axis=1)
    grad_in = jnp.stack([in_sum.astype(f32), in_key, in_value]).transpose(1, 0, 2)

    taps_at = 2 * poles
    gain_at = taps_at + 9
    return (
        output.reshape(tokens.shape),
        grad_tokens.reshape(tokens.shape),
        grad_gain_mix,
        grad_in,
        small[taps_at:gain_at].reshape(3, 3, channels),
        small[:poles],
        small[poles:taps_at],
        grad_out.T,
        small[gain_at : gain_at + gain_rows].reshape(width),
        grad_gu_w,
        grad_down,
    )


def solution(mesh):
    in_specs = (
        P(None, "seq", None),
        P(),
        P(None, "seq"),
        P(),
        P(None, None, "tp"),
        P(None, None, "tp"),
        P(None, "tp"),
        P(None, "tp"),
        P("tp", None),
        P(),
        P(None, None, "tp"),
        P("tp", None),
        P(None, "seq", None),
    )
    out_specs = (
        P(None, "seq", None),
        P(None, "seq", None),
        P(),
        P("seq", None, "tp"),
        P(None, None, "tp"),
        P(None, "tp"),
        P(None, "tp"),
        P("tp", "seq"),
        P(),
        P("seq", None, "tp"),
        P("tp", "seq"),
    )
    return jax.shard_map(
        functools.partial(shards, mesh.shape["seq"]),
        mesh=mesh,
        in_specs=in_specs,
        out_specs=out_specs,
        check_vma=False,
    )
```
